32 devices in a mesh: tp: 8 (over z, y), ep: 4 (over x, core).
Axes of the slice: x: 2, y: 2, z: 4, core: 2. Of those that a mesh axis runs over, the one named last changes fastest.
Arguments:
- attn_out: bfloat16 [4096, 8192], P('ep', 'tp'), may hold values from -6 to 6
- residual: bfloat16 [4096, 7168], P(('ep', 'tp')), may hold values from -6 to 6
- w_out: bfloat16 [8192, 7168], P('tp'), may hold values from -0.0625 to 0.0625
- norm_gain: bfloat16 [7168], replicated, may hold values from 0.5 to 1.5
- router: bfloat16 [7168, 256], P(None, 'tp'), may hold values from -0.0625 to 0.0625
- router_bias: float32 [256], replicated, may hold values from -3 to 3
- choices: int32 [4096, 8], P(('ep', 'tp')), may hold values from 0 to 255, as said below
- w_gate: bfloat16 [8, 7168, 2048], P('tp', None, 'ep'), may hold values from -0.0625 to 0.0625
- w_up: bfloat16 [8, 7168, 2048], P('tp', None, 'ep'), may hold values from -0.0625 to 0.0625
- w_down: bfloat16 [8, 2048, 7168], P('tp', 'ep'), may hold values from -0.125 to 0.125
Outputs:
- hidden_out: bfloat16 [4096, 7168], P(('ep', 'tp'))
- moe_out: bfloat16 [4096, 7168], P(('ep', 'tp'))
- load: float32 [256], replicated
- bias_next: float32 [256], replicated
The draws below stay inside these ranges and needn't reach their ends.
Inputs may be any that keep to these rules, and one draw needn't show every extreme that they name: `choices`: each row names 8 different experts. Among the rows of one device no expert below 8 is named by more than 2 rows; one such expert is named by exactly 2 rows of every device.
All inputs are finite; a program needn't handle non-finite values.
Results may differ from the reference program's by a relative error of at most 0.034.
Values may be sent and summed in bfloat16 or wider, within the bound.
No kernel may reach another device: no remote copies, remote signals or barrier semaphores. Data moves between devices by JAX's collectives and lax.ppermute only.
A program may use at most 128 MiB of HBM per device.

```python
import jax
import jax.numpy as jnp
from jax import lax

D = 7168
HEADS = 64
HD = 128
FF = 2048
ROUTED = 256
TOP = 8
TOK_DEV = 128
CAP = 2
FLIGHT = 8
TOKENS = 4096
N_TP = 8
N_EP = 4


def draw_choices(key, part):
    key = jax.random.fold_in(key, 7)
    key_hot, key_level, key_count, key_order, key_rest, key_favour, key_pull, key_group, key_lean = jax.random.split(key, 9)
    blocks = TOKENS // TOK_DEV
    hottest = jax.random.randint(key_hot, (), 0, FLIGHT)
    rising = 1 + 3 * jnp.arange(blocks, dtype=jnp.int32) // blocks
    levels = jax.random.randint(key_level, (FLIGHT,), 1, 5)
    ceiling = jnp.minimum(CAP, levels[None, :] * rising[:, None] * CAP // 8 + 1)
    counts = jax.random.randint(key_count, (blocks, FLIGHT), 0, ceiling + 1)
    counts = jnp.where(jnp.arange(FLIGHT)[None, :] == hottest, CAP, counts)
    orders = jax.random.permutation(key_order, jnp.broadcast_to(jnp.arange(TOK_DEV, dtype=jnp.int32), (blocks, TOK_DEV)), axis=1, independent=True)
    shifted = (orders[:, :, None] - CAP * jnp.arange(FLIGHT, dtype=jnp.int32)[None, None, :]) % TOK_DEV
    member = (shifted < counts[:, None, :]).reshape(TOKENS, FLIGHT)
    window_ids = jnp.where(member, jnp.arange(FLIGHT, dtype=jnp.int32)[None, :], ROUTED + FLIGHT)
    window_ids = jnp.sort(window_ids, axis=1)
    chosen_count = jnp.sum(member.astype(jnp.int32), axis=1)
    ranking = jax.random.randint(key_rest, (TOKENS, ROUTED), 0, 1048576) * ROUTED + jnp.arange(ROUTED, dtype=jnp.int32)[None, :]
    block_ids = jnp.arange(blocks, dtype=jnp.int32)
    blocks_ep = blocks // FLIGHT
    position = block_ids % FLIGHT * blocks_ep + block_ids // FLIGHT
    token_block = jnp.arange(TOKENS, dtype=jnp.int32) // TOK_DEV
    expert_ids = jnp.arange(ROUTED, dtype=jnp.int32)
    rest_order = jax.random.permutation(key_group, ROUTED - FLIGHT).astype(jnp.int32)
    coin = jax.random.randint(jax.random.fold_in(key_group, 1), (ROUTED - FLIGHT,), 0, 2)
    rest_group = jnp.where(rest_order < TOP, 1, jnp.where(rest_order < 2 * TOP, 0, coin))
    group = jnp.concatenate([jnp.zeros((FLIGHT,), jnp.int32), rest_group.astype(jnp.int32)])
    lean_level = 1 + 8 * position // blocks
    lean = (jax.random.randint(key_lean, (TOKENS,), 0, 10) < lean_level[token_block]).astype(jnp.int32)
    ranking = ranking + jnp.where(group[None, :] == lean[:, None], 268435456, 0)
    ranking = jnp.where(expert_ids[None, :] < FLIGHT, -1, ranking)
    favoured = jax.random.randint(key_favour, (), FLIGHT, ROUTED)
    threshold = 1 + 9 * position // (2 * blocks)
    pulled = jax.random.randint(key_pull, (TOKENS,), 0, 12) < threshold[token_block]
    boost = jnp.where(pulled[:, None] & (expert_ids[None, :] == favoured), 1073741824, 0)
    ranking = jnp.where(boost > 0, boost, ranking)
    others = lax.top_k(ranking, TOP)[1].astype(jnp.int32)
    joined = jnp.concatenate([window_ids[:, :TOP].astype(jnp.int32), others], axis=1)
    place = jnp.arange(TOP, dtype=jnp.int32)[None, :]
    pick = jnp.where(place < chosen_count[:, None], place, TOP + place - chosen_count[:, None])
    return jnp.take_along_axis(joined, pick, axis=1).astype(jnp.int32)


def shard_levels(key, dims, shards, smallest, high):
    factor_of = 1.0
    for dim, shards_of in shards:
        steps = jax.random.uniform(jax.random.fold_in(jax.random.fold_in(key, 6), dim), (shards_of,), jnp.float32, smallest / len(shards), high / len(shards))
        factor_of = factor_of * jnp.repeat(jnp.exp(steps), dims[dim] // shards_of).reshape((-1,) + (1,) * (len(dims) - 1 - dim))
    return factor_of


def noise(own_key, dims, spread, bound, cuts=(), kind=jnp.bfloat16):
    drawn = spread * jax.random.normal(own_key, dims, jnp.float32)
    if cuts:
        drawn = drawn * shard_levels(own_key, dims, cuts, -0.22, 0.18)
    return jnp.clip(drawn, -bound, bound).astype(kind)


def setup_inputs(seed: int = 0) -> dict:
    splits = jax.random.split(jax.random.key(seed), 11)
    attn_out = noise(splits[0], (TOKENS, HEADS * HD), 1.0, 6.0, ((0, 4), (1, 8)))
    residual = noise(splits[1], (TOKENS, D), 1.0, 6.0, ((0, 32),))
    w_out = noise(splits[2], (HEADS * HD, D), (HEADS * HD) ** -0.5, 0.0625, ((0, 8),))
    norm_gain = jnp.clip(1.0 + 0.1 * jax.random.normal(splits[3], (D,), jnp.float32), 0.5, 1.5).astype(jnp.bfloat16)
    router = noise(splits[4], (D, ROUTED), D ** -0.5, 0.0625, ((1, 8),))
    router_bias = noise(splits[5], (ROUTED,), 0.2, 3.0, (), jnp.float32)
    choices = draw_choices(jax.random.fold_in(splits[10], 71), 0)
    w_gate = noise(splits[7], (FLIGHT, D, FF), D ** -0.5, 0.0625, ((0, 8), (2, 4)))
    w_up = noise(splits[8], (FLIGHT, D, FF), D ** -0.5, 0.0625, ((0, 8), (2, 4)))
    w_down = noise(splits[9], (FLIGHT, FF, D), FF ** -0.5, 0.125, ((0, 8), (1, 4)))
    return {"attn_out": attn_out, "residual": residual, "w_out": w_out, "norm_gain": norm_gain, "router": router, "router_bias": router_bias, "choices": choices, "w_gate": w_gate, "w_up": w_up, "w_down": w_down}


norm_eps = 1e-06
route_scale = 2.5
bias_rate = 0.001

def reference(attn_out, residual, w_out, norm_gain, router, router_bias, choices, w_gate, w_up, w_down):
    head_cols = HEADS * HD // N_TP
    projected = jnp.zeros(residual.shape, jnp.float32)
    for head_group in range(N_TP):
        part_cols = attn_out[:, head_group * head_cols:(head_group + 1) * head_cols]
        part_rows = w_out[head_group * head_cols:(head_group + 1) * head_cols]
        partial_value = jnp.dot(part_cols, part_rows, preferred_element_type=jnp.float32).astype(jnp.bfloat16)
        partial_value = lax.optimization_barrier(partial_value)
        projected = projected + partial_value.astype(jnp.float32)
    hidden_out = (residual.astype(jnp.float32) + projected).astype(jnp.bfloat16)
    stream = hidden_out.astype(jnp.float32)
    scaled = stream * lax.rsqrt(lax.optimization_barrier(jnp.mean(stream * stream, axis=-1, keepdims=True)) + norm_eps)
    normed = (scaled * norm_gain.astype(jnp.float32)).astype(jnp.bfloat16)
    scores = jax.nn.sigmoid(jnp.dot(normed, router, preferred_element_type=jnp.float32))
    chosen = jnp.take_along_axis(scores, choices, axis=1)
    weights = route_scale * chosen / lax.optimization_barrier(jnp.sum(chosen, axis=-1, keepdims=True))
    flight_ids = jnp.arange(FLIGHT, dtype=jnp.int32)
    matches = choices[:, :, None] == flight_ids[None, None, :]
    expert_weight = lax.optimization_barrier(jnp.sum(jnp.where(matches, weights[:, :, None], 0.0), axis=1))
    member = jnp.any(matches, axis=1).astype(jnp.int32)
    devices = N_TP * N_EP
    slots = devices * CAP
    blocked = member.reshape(devices, TOK_DEV, FLIGHT)
    slot_rank = (jnp.cumsum(blocked, axis=1) - blocked).reshape(TOKENS, FLIGHT)
    block_of = jnp.arange(TOKENS, dtype=jnp.int32) // TOK_DEV
    mixed = jnp.zeros(residual.shape, jnp.float32)
    for expert in range(FLIGHT):
        target = jnp.where(member[:, expert] == 1, block_of * CAP + slot_rank[:, expert], slots).astype(jnp.int32)
        buffer = jnp.zeros((slots + 1, D), jnp.bfloat16).at[target].set(normed)[:slots]
        gate_val = jnp.dot(buffer, w_gate[expert], preferred_element_type=jnp.float32)
        up_val = jnp.dot(buffer, w_up[expert], preferred_element_type=jnp.float32)
        active = (jax.nn.silu(gate_val) * up_val).astype(jnp.bfloat16)
        output = jnp.dot(active, w_down[expert], preferred_element_type=jnp.float32).astype(jnp.bfloat16)
        fetched = jnp.concatenate([output, jnp.zeros((1, D), jnp.bfloat16)], axis=0)[target]
        mixed = mixed + expert_weight[:, expert:expert + 1] * fetched.astype(jnp.float32)
    moe_out = mixed.astype(jnp.bfloat16)
    counts = jnp.zeros((ROUTED,), jnp.int32).at[choices.reshape(-1)].add(1)
    load = counts.astype(jnp.float32) * ROUTED / (TOKENS * TOP)
    bias_next = router_bias + bias_rate * jnp.sign(TOKENS * TOP - counts * ROUTED).astype(jnp.float32)
    return (hidden_out, moe_out, load, bias_next)
```

```python
import jax
import jax.numpy as jnp
from jax import lax
from jax.experimental import pallas as pl
from jax.experimental.pallas import tpu as pltpu
from jax.sharding import PartitionSpec as P

TOP = 8
CAP = 2


norm_eps = 1e-06
route_scale = 2.5
bias_rate = 0.001
f32 = jnp.float32
bf16 = jnp.bfloat16


def swap(value, axis, bit):
    size = lax.axis_size(axis)
    return lax.ppermute(value, axis, [(i, i ^ bit) for i in range(size)])


def bits_of(size):
    return [1 << k for k in range(size.bit_length() - 1)]


def halving_order(stages):
    order = [0]
    for bit in reversed(stages):
        order = order + [j | bit for j in order]
    return order


ANY = pl.BlockSpec(memory_space=pl.ANY)


def run(body, grid, ins, outs, marks, aliases=None, scratch=(), mib=16):
    count, skip = len(ins), len(marks)

    def inner(*refs):
        body(*refs[:count], *refs[count + skip :])

    return pl.pallas_call(
        inner,
        grid=grid,
        in_specs=[spec for _, spec in ins] + [ANY] * skip,
        out_specs=[spec for _, spec in outs],
        out_shape=[jax.ShapeDtypeStruct(shape, kind) for (shape, kind), _ in outs],
        input_output_aliases=aliases or {},
        scratch_shapes=list(scratch),
        compiler_params=pltpu.CompilerParams(vmem_limit_bytes=mib * 1024 * 1024),
        cost_estimate=pl.CostEstimate(flops=1, bytes_accessed=1, transcendentals=0),
    )(*[a for a, _ in ins], *marks)


def whole(shape):
    return pl.BlockSpec(shape, lambda i: (0,) * len(shape))


def kept_block(shape):
    return pl.BlockSpec(shape, lambda i: (0,) * len(shape), pipeline_mode=pl.Buffered(1))


def block_of(span, most):
    size = span.stop - span.start
    best = 128
    for n in range(128, most + 1, 128):
        if size % n == 0 and span.start % n == 0:
            best = n
    return best


def gated(value, marks):
    return run(lambda *refs: None, (1,), [(value, ANY)], [((value.shape, value.dtype), ANY)], marks, {0: 0})[0]


def adds(groups, marks):
    rows = groups[0][0][0].shape[0]
    cut = rows // 2
    plain = all(len(group) == 1 for group in groups)
    sizes = {kept.shape[1] for group in groups for kept, _ in group}
    wide = block_of(slice(0, min(sizes)), 640) if plain and len(sizes) == 1 and cut >= 128 else None
    ins, outs = [], []
    for group in groups:
        cols = sum(kept.shape[1] for kept, _ in group)
        for pair in group:
            for value in pair:
                ins.append((value, pl.BlockSpec((rows, wide), lambda i: (0, i)) if wide else whole(value.shape)))
        for kind in (bf16, f32):
            spec = pl.BlockSpec((cut, wide), lambda i: (0, i)) if wide else whole((cut, cols))
            outs.append((((cut, cols), kind), spec))
    counts = [len(group) for group in groups]

    def body(*refs):
        place, out_place = 0, 2 * sum(counts)
        for count in counts:
            out, rest = refs[out_place], refs[out_place + 1]
            low = 0
            for _ in range(count):
                kept, got = refs[place], refs[place + 1]
                size = kept.shape[1]
                out[:, low : low + size] = (kept[cut:].astype(f32) + got[cut:].astype(f32)).astype(bf16)
                rest[:, low : low + size] = kept[:cut].astype(f32) + got[:cut].astype(f32)
                low += size
                place += 2
            out_place += 2

    got = run(body, (min(sizes) // wide if wide else 1,), ins, outs, marks)
    return [(got[2 * n], got[2 * n + 1]) for n in range(len(groups))]


def mm(a, b):
    return jnp.dot(a, b, preferred_element_type=f32)


def mm_t(a, b):
    return lax.dot_general(a, b, (((1,), (1,)), ((), ())), preferred_element_type=f32)


def mm_rows(a, b):
    return lax.dot_general(a, b, (((0,), (0,)), ((), ())), preferred_element_type=f32)


def on_device(
    attn_out, residual, w_out, norm_gain, router, router_bias, choices, w_gate, w_up, w_down
):
    tp_count = lax.axis_size("tp")
    ep_count = lax.axis_size("ep")
    tok_rows = residual.shape[0]
    width = residual.shape[1]
    routed = router_bias.shape[0]
    top = choices.shape[1]
    all_rows = tp_count * tok_rows
    first = CAP * tp_count
    me = lax.axis_index("tp")
    ep_me = lax.axis_index("ep")
    tp_bits, ep_bits = bits_of(tp_count), bits_of(ep_count)
    y_first = list(tp_bits)
    z_first = [tp_bits[1], tp_bits[0]] + tp_bits[2:]
    far = tp_bits[2:]
    stages = {"y": y_first, "z": z_first}
    order = {"y": halving_order(y_first), "z": halving_order(z_first)}
    half = all_rows // 2
    flying, values, hidden = {}, {}, []

    onehot = choices[:, :, None] == jnp.arange(routed, dtype=jnp.int32)
    counts = jnp.sum(onehot.astype(jnp.int32), axis=(0, 1))
    count_hops = list(ep_bits)
    rel = [0]
    for bit in tp_bits[::-1]:
        rel = rel + [j | bit for j in rel]
    per_device = routed // tp_count
    per_part = per_device // ep_count
    part_rows = -(-(per_part + 2) // 16) * 16
    base_digit = 64

    def count_hop():
        nonlocal counts
        counts = counts + swap(counts, "ep", count_hops.pop(0))
        return [counts]

    def router_gather(marks):
        part = lax.dynamic_slice_in_dim(router.T, ep_me * per_part, per_part, axis=0)
        digits = jnp.stack([counts // base_digit, counts % base_digit]).astype(bf16)
        digits = jnp.pad(digits, ((0, part_rows - per_part - 2), (0, width - routed)))
        part = gated(jnp.concatenate([part, digits], axis=0), marks)
        for bit in tp_bits[::-1]:
            part = jnp.concatenate([part, swap(part, "tp", bit)], axis=0)
        return part

    blocks = [
        lax.dynamic_slice_in_dim(attn_out, (me ^ j) * tok_rows, tok_rows, axis=0)
        for j in range(tp_count)
    ]
    halves = []
    for kind in ("y", "z"):
        for part in (slice(0, tp_count // 2), slice(tp_count // 2, tp_count)):
            halves.append(jnp.concatenate([blocks[j] for j in order[kind][part]], axis=0))
    tiles = {"y0": 2, "z0": 2, "y1": 4, "y2": 4, "y3": 5, "z1": 3, "y4": 4, "y5": 2, "z2": 2}
    unit = width // sum(tiles.values())
    spans, lo = {}, 0
    for name, count in tiles.items():
        spans[name] = slice(lo, lo + count * unit)
        lo += count * unit
    partial = {}

    def bulk(names, marks):
        base = spans[names[0]].start // unit
        starts = [spans[name].start // unit - base for name in names]
        outs = []
        for name, low in zip(names, starts):
            top_block = tiles[name] - 1
            spec = pl.BlockSpec(
                (half, unit), lambda i, low=low, top_block=top_block: (0, jnp.clip(i - low, 0, top_block))
            )
            outs += [(((half, tiles[name] * unit), bf16), spec)] * 2

        def body(*refs):
            step = pl.program_id(0)
            w, refs_out = refs[4], refs[5:]
            for n, (name, low) in enumerate(zip(names, starts)):

                @pl.when((step >= low) & (step < low + tiles[name]))
                def _(n=n, name=name):
                    at = 0 if name[0] == "y" else 2
                    refs_out[2 * n][...] = mm(refs[at][...], w[...]).astype(bf16)
                    refs_out[2 * n + 1][...] = mm(refs[at + 1][...], w[...]).astype(bf16)

        got = run(
            body,
            (sum(tiles[name] for name in names),),
            [(rows, kept_block(rows.shape)) for rows in halves]
            + [(w_out, pl.BlockSpec((w_out.shape[0], unit), lambda i: (0, base + i)))],
            outs,
            marks,
            mib=50,
        )
        for n, name in enumerate(names):
            partial[name] = (got[2 * n], got[2 * n + 1])
        return [got[-2]]

    def begin(name, marks=None):
        kept, out = partial.pop(name)
        if marks:
            out = gated(out, marks)
        flying[name] = swap(out, "tp", stages[name[0]][0])
        values[name] = kept

    def second(names, marks):
        parts = adds([[(values.pop(name), flying.pop(name))] for name in names], marks)
        for name, (out, kept) in zip(names, parts):
            flying[name] = swap(out, "tp", stages[name[0]][1])
            values[name] = kept
        return [parts[0][0]]

    def third(names, marks):
        ((out, kept),) = adds([[(values.pop(name), flying.pop(name)) for name in names]], marks)
        flying[names] = swap(out, "tp", far[0])
        values[names] = kept
        return [out]

    def finish(names, marks):
        kept, got = values.pop(names), flying.pop(names)
        for bit in far[1:]:
            ((out, kept),) = adds([[(kept, got)]], marks)
            got = swap(out, "tp", bit)
        span = slice(spans[names[0]].start, spans[names[-1]].stop)
        wide = block_of(span, 1280)
        low = span.start // wide
        here = pl.BlockSpec((tok_rows, wide), lambda i: (0, low + i))
        part = pl.BlockSpec((tok_rows, wide), lambda i: (0, i))

        def body(kept, got, residual, *refs):
            refs[-2][...] = (residual[...].astype(f32) + (kept[...] + got[...].astype(f32))).astype(bf16)
            refs[-1][...] = jnp.zeros((8, 128), f32)

        before = [(hidden.pop(), ANY)] if hidden else []
        out, mark = run(
            body,
            ((span.stop - span.start) // wide,),
            [(kept, part), (got, part), (residual, here)] + before,
            [(((tok_rows, width), bf16), here), (((8, 128), f32), whole((8, 128)))],
            marks,
            {3: 0} if before else None,
        )
        hidden.append(out)
        return [mark]

    marks = bulk(("y0", "z0"), [])
    begin("y0")
    begin("z0")
    marks = bulk(("y1",), marks)
    marks = second(("y0", "z0"), marks)
    begin("y1", marks)
    marks = bulk(("y2",), marks)
    marks = second(("y1",), marks + count_hop())
    begin("y2", marks)
    marks = third(("y0", "z0"), marks)
    marks = bulk(("y3", "z1"), marks)
    begin("y3")
    marks = third(("y1",), marks)
    begin("z1", marks)
    marks = finish(("y0", "z0"), marks + count_hop())
    marks = second(("y2",), marks)
    marks = bulk(("y4",), marks)
    begin("y4")
    marks = finish(("y1",), marks)
    marks = second(("z1",), marks)
    marks = third(("y2",), marks)
    marks = second(("y3",), marks)
    marks = bulk(("y5", "z2"), marks)
    begin("y5")
    begin("z2")
    marks = finish(("y2",), marks)
    marks = third(("y3",), marks)
    marks = second(("y4",), marks)
    marks = third(("z1",), marks)
    marks = finish(("y3",), marks)
    marks = second(("z2",), marks)
    marks = third(("y4",), marks)
    marks = second(("y5",), marks)
    marks = finish(("z1",), marks)
    router_all = router_gather(marks)
    marks = finish(("y4",), marks)
    marks = third(("y5", "z2"), marks)
    finish(("y5", "z2"), marks)
    (hidden_out,) = hidden

    window = onehot[:, :, :tp_count]
    member = jnp.any(window, axis=1).astype(jnp.int32)
    slot_rank = jnp.cumsum(member, axis=0) - member
    slot_ids = jnp.arange(CAP, dtype=jnp.int32)[None, :, None]
    slot_pick = (member.T[:, None, :] == 1) & (slot_rank.T[:, None, :] == slot_ids)
    pick = slot_pick.reshape(first, tok_rows).astype(bf16)

    lanes = 128
    choice_cols = jnp.pad(choices.astype(bf16), ((0, 0), (0, lanes - top)))

    def norm_body(pick, rows, gain, choice, out):
        stream = mm(pick[...], rows[...])
        scaled = stream * lax.rsqrt(jnp.mean(stream * stream, axis=-1, keepdims=True) + norm_eps)
        out[:, :width] = (scaled * gain[...].astype(f32)).astype(bf16)
        out[:, width:] = mm(pick[...], choice[...]).astype(bf16)

    (normed,) = run(
        norm_body,
        (1,),
        [
            (pick, whole(pick.shape)),
            (hidden_out, whole(hidden_out.shape)),
            (norm_gain[None], whole((1, width))),
            (choice_cols, whole(choice_cols.shape)),
        ],
        [(((first, width + lanes), bf16), whole((first, width + lanes)))],
        [],
    )
    landed = lax.all_to_all(
        normed.reshape(tp_count, CAP, width + lanes), "tp", split_axis=0, concat_axis=0, tiled=True
    ).reshape(first, width + lanes)
    picked = [landed]
    for bit in ep_bits[::-1]:
        picked = picked + [swap(rows, "ep", bit) for rows in picked]
    rows_all = first * ep_count
    hid = w_gate.shape[2]
    deep = block_of(slice(0, width), 1024)
    last_step = width // deep - 1

    def up_body(*refs):
        rows, (gate_w, up_w, out, gate_sum, up_sum) = refs[:ep_count], refs[ep_count:]
        step = pl.program_id(0)

        @pl.when(step == 0)
        def _():
            gate_sum[...] = jnp.zeros_like(gate_sum)
            up_sum[...] = jnp.zeros_like(up_sum)

        x = jnp.concatenate([r[...] for r in rows], axis=0)
        gate_sum[...] += mm(x, gate_w[0])
        up_sum[...] += mm(x, up_w[0])

        @pl.when(step == last_step)
        def _():
            gate = gate_sum[...]
            out[...] = (gate / (1.0 + jnp.exp(-gate)) * up_sum[...]).astype(bf16)

    deep_rows = pl.BlockSpec((first, deep), lambda i: (0, i))
    deep_w = pl.BlockSpec((1, deep, hid), lambda i: (0, i, 0))
    (active,) = run(
        up_body,
        (last_step + 1,),
        [(rows, deep_rows) for rows in picked] + [(w_gate, deep_w), (w_up, deep_w)],
        [(((rows_all, hid), bf16), whole((rows_all, hid)))],
        [],
        scratch=[pltpu.VMEM((rows_all, hid), f32)] * 2,
    )
    cut = rows_all // 2

    def down_body(x, w, out, kept):
        value = mm(x[...], w[0])
        kept[...] = value[:cut]
        out[...] = value[cut:].astype(bf16)

    wide_half = pl.BlockSpec((cut, deep), lambda i: (0, i))
    out, kept = run(
        down_body,
        (last_step + 1,),
        [(active, whole(active.shape)), (w_down, pl.BlockSpec((1, hid, deep), lambda i: (0, 0, i)))],
        [(((cut, width), bf16), wide_half), (((cut, width), f32), wide_half)],
        [],
    )
    got = swap(out, "ep", ep_bits[0])

    row_of = jnp.arange(part_rows, dtype=jnp.int32)
    column_ids = (jnp.array(rel, jnp.int32) ^ me)[:, None] * per_device + ep_me * per_part + row_of
    column_ids = jnp.where(row_of < per_part, column_ids, -1).reshape(1, -1)

    def score_body(*refs):
        rows, (table, columns, expert, out) = refs[:ep_count], refs[ep_count:]
        x = jnp.concatenate([r[:, :width] for r in rows], axis=0)
        ids = jnp.concatenate([r[:, width:] for r in rows], axis=0).astype(f32).astype(jnp.int32)
        scores = 1.0 / (1.0 + jnp.exp(-mm_t(x, table[...])))
        here = columns[...]
        chosen = jnp.where(here == expert[...], scores, 0.0)
        total = jnp.zeros_like(scores)
        for k in range(top):
            total += jnp.where(here == ids[:, k : k + 1], scores, 0.0)
        lane = lax.broadcasted_iota(jnp.int32, out.shape, 1)
        chosen = jnp.sum(chosen, axis=-1, keepdims=True)
        total = jnp.sum(total, axis=-1, keepdims=True)
        out[...] = jnp.where(lane == 0, chosen, jnp.where(lane == 1, total, 0.0))

    expert_id = jnp.full((1, 1), me, jnp.int32)
    (parts,) = run(
        score_body,
        (1,),
        [(rows, whole(rows.shape)) for rows in picked]
        + [
            (router_all, whole(router_all.shape)),
            (column_ids, whole(column_ids.shape)),
            (expert_id, whole((1, 1))),
        ],
        [(((rows_all, lanes), f32), whole((rows_all, lanes)))],
        [],
    )
    for bit in ep_bits:
        low = parts.shape[0] // 2
        parts = parts[:low] + swap(parts[low:], "ep", bit)
    for bit in ep_bits[1:]:
        ((out, kept),) = adds([[(kept, got)]], [])
        got = swap(out, "ep", bit)

    def weigh_body(kept, got, part, out):
        value = (kept[...] + got[...].astype(f32)).astype(bf16).astype(f32)
        out[...] = (value * (route_scale * part[:, 0:1] / part[:, 1:2])).astype(bf16)

    (summed,) = run(
        weigh_body,
        (1,),
        [(kept, whole(kept.shape)), (got, whole(kept.shape)), (parts, whole(parts.shape))],
        [((kept.shape, bf16), whole(kept.shape))],
        [],
    )
    returned = lax.all_to_all(
        summed.reshape(tp_count, CAP, width), "tp", split_axis=0, concat_axis=0, tiled=True
    ).reshape(first, width)
    moe_out = mm_rows(pick, returned).astype(bf16)

    digits = router_all.reshape(tp_count, part_rows, width)[:, per_part : per_part + 2, :routed]
    digits = jnp.sum(digits.astype(jnp.int32), axis=0)
    counts = digits[0] * base_digit + digits[1]
    all_slots = all_rows * ep_count * top
    load = counts.astype(f32) * routed / all_slots
    bias_next = router_bias + bias_rate * jnp.sign(all_slots - counts * routed).astype(f32)
    return (hidden_out, moe_out, load, bias_next)


def solution(mesh):
    placed = (
        P("ep", "tp"),
        P(("ep", "tp"), None),
        P("tp", None),
        P(),
        P(None, "tp"),
        P(),
        P(("ep", "tp"), None),
        P("tp", None, "ep"),
        P("tp", None, "ep"),
        P("tp", "ep", None),
    )
    return jax.shard_map(
        on_device,
        mesh=mesh,
        in_specs=placed,
        out_specs=(P(("ep", "tp"), None), P(("ep", "tp"), None), P(), P()),
        check_vma=False,
    )
```

```python
import jax
import jax.numpy as jnp
from jax import lax
from jax.experimental import pallas as pl
from jax.experimental.pallas import tpu as pltpu
from jax.sharding import PartitionSpec as P

TOP = 8
CAP = 2


norm_eps = 1e-06
route_scale = 2.5
bias_rate = 0.001
f32 = jnp.float32
bf16 = jnp.bfloat16


def swap(value, axis, bit):
    size = lax.axis_size(axis)
    return lax.ppermute(value, axis, [(i, i ^ bit) for i in range(size)])


def bits_of(size):
    return [1 << k for k in range(size.bit_length() - 1)]


def halving_order(stages):
    order = [0]
    for bit in reversed(stages):
        order = order + [j | bit for j in order]
    return order


ANY = pl.BlockSpec(memory_space=pl.ANY)


def run(body, grid, ins, outs, marks, aliases=None, scratch=(), mib=16, moved=1):
    count, skip = len(ins), len(marks)

    def inner(*refs):
        body(*refs[:count], *refs[count + skip :])

    return pl.pallas_call(
        inner,
        grid=grid,
        in_specs=[spec for _, spec in ins] + [ANY] * skip,
        out_specs=[spec for _, spec in outs],
        out_shape=[jax.ShapeDtypeStruct(shape, kind) for (shape, kind), _ in outs],
        input_output_aliases=aliases or {},
        scratch_shapes=list(scratch),
        compiler_params=pltpu.CompilerParams(vmem_limit_bytes=mib * 1024 * 1024),
        cost_estimate=pl.CostEstimate(flops=1, bytes_accessed=moved, transcendentals=0),
    )(*[a for a, _ in ins], *marks)


def whole(shape):
    return pl.BlockSpec(shape, lambda i: (0,) * len(shape))


def kept_block(shape):
    return pl.BlockSpec(shape, lambda i: (0,) * len(shape), pipeline_mode=pl.Buffered(1))


def block_of(span, most):
    size = span.stop - span.start
    best = 128
    for n in range(128, most + 1, 128):
        if size % n == 0 and span.start % n == 0:
            best = n
    return best


def gated(value, marks):
    return run(lambda *refs: None, (1,), [(value, ANY)], [((value.shape, value.dtype), ANY)], marks, {0: 0})[0]


def adds(groups, marks):
    rows = groups[0][0][0].shape[0]
    cut = rows // 2
    plain = all(len(group) == 1 for group in groups)
    sizes = {kept.shape[1] for group in groups for kept, _ in group}
    wide = block_of(slice(0, min(sizes)), 640) if plain and len(sizes) == 1 and cut >= 128 else None
    ins, outs = [], []
    for group in groups:
        cols = sum(kept.shape[1] for kept, _ in group)
        for pair in group:
            for value in pair:
                ins.append((value, pl.BlockSpec((rows, wide), lambda i: (0, i)) if wide else whole(value.shape)))
        for kind in (bf16, f32):
            spec = pl.BlockSpec((cut, wide), lambda i: (0, i)) if wide else whole((cut, cols))
            outs.append((((cut, cols), kind), spec))
    counts = [len(group) for group in groups]

    def body(*refs):
        place, out_place = 0, 2 * sum(counts)
        for count in counts:
            out, rest = refs[out_place], refs[out_place + 1]
            low = 0
            for _ in range(count):
                kept, got = refs[place], refs[place + 1]
                size = kept.shape[1]
                out[:, low : low + size] = (kept[cut:].astype(f32) + got[cut:].astype(f32)).astype(bf16)
                rest[:, low : low + size] = kept[:cut].astype(f32) + got[:cut].astype(f32)
                low += size
                place += 2
            out_place += 2

    got = run(body, (min(sizes) // wide if wide else 1,), ins, outs, marks)
    return [(got[2 * n], got[2 * n + 1]) for n in range(len(groups))]


def mm(a, b):
    return jnp.dot(a, b, preferred_element_type=f32)


def mm_t(a, b):
    return lax.dot_general(a, b, (((1,), (1,)), ((), ())), preferred_element_type=f32)


def mm_rows(a, b):
    return lax.dot_general(a, b, (((0,), (0,)), ((), ())), preferred_element_type=f32)


def on_device(
    attn_out, residual, w_out, norm_gain, router, router_bias, choices, w_gate, w_up, w_down
):
    tp_count = lax.axis_size("tp")
    ep_count = lax.axis_size("ep")
    tok_rows = residual.shape[0]
    width = residual.shape[1]
    routed = router_bias.shape[0]
    top = choices.shape[1]
    all_rows = tp_count * tok_rows
    first = CAP * tp_count
    me = lax.axis_index("tp")
    ep_me = lax.axis_index("ep")
    tp_bits, ep_bits = bits_of(tp_count), bits_of(ep_count)
    y_first = list(tp_bits)
    z_first = [tp_bits[1], tp_bits[0]] + tp_bits[2:]
    far = tp_bits[2:]
    stages = {"y": y_first, "z": z_first}
    order = {"y": halving_order(y_first), "z": halving_order(z_first)}
    half = all_rows // 2
    flying, values, hidden = {}, {}, []

    onehot = choices[:, :, None] == jnp.arange(routed, dtype=jnp.int32)
    counts = jnp.sum(onehot.astype(jnp.int32), axis=(0, 1))
    count_hops = list(ep_bits)
    rel = [0]
    for bit in tp_bits[::-1]:
        rel = rel + [j | bit for j in rel]
    per_device = routed // tp_count
    per_part = per_device // ep_count
    digit_cols = -(-2 * routed // (per_part * 128)) * 128
    base_digit = 64

    def count_hop():
        nonlocal counts
        counts = counts + swap(counts, "ep", count_hops.pop(0))
        return [counts]

    def router_payload():
        part = lax.dynamic_slice_in_dim(router.T, ep_me * per_part, per_part, axis=0)
        digits = jnp.concatenate([counts // base_digit, counts % base_digit]).astype(bf16)
        digits = jnp.pad(digits, (0, per_part * digit_cols - 2 * routed)).reshape(per_part, digit_cols)
        return jnp.concatenate([part, digits], axis=1)

    def router_gather(part, marks):
        part = gated(part, marks)
        for bit in tp_bits[::-1]:
            part = jnp.concatenate([part, swap(part, "tp", bit)], axis=0)
        return part

    blocks = [
        lax.dynamic_slice_in_dim(attn_out, (me ^ j) * tok_rows, tok_rows, axis=0)
        for j in range(tp_count)
    ]
    halves = {
        kind: [
            jnp.concatenate([blocks[j] for j in order[kind][part]], axis=0)
            for part in (slice(0, tp_count // 2), slice(tp_count // 2, tp_count))
        ]
        for kind in ("y", "z")
    }
    tiles = {"y0": 2, "z0": 4, "y1": 4, "y2": 6, "y3": 5, "y4": 4, "y5": 3}
    unit = width // sum(tiles.values())
    spans, lo = {}, 0
    for name, count in tiles.items():
        spans[name] = slice(lo, lo + count * unit)
        lo += count * unit
    partial = {}

    def bulk(names, marks):
        base = spans[names[0]].start // unit
        starts = [spans[name].start // unit - base for name in names]
        outs = []
        for name, low in zip(names, starts):
            top_block = tiles[name] - 1
            spec = pl.BlockSpec(
                (half, unit), lambda i, low=low, top_block=top_block: (0, jnp.clip(i - low, 0, top_block))
            )
            outs += [(((half, tiles[name] * unit), bf16), spec)] * 2

        kinds = sorted({name[0] for name in names})
        rows_used = [rows for kind in kinds for rows in halves[kind]]

        def body(*refs):
            step = pl.program_id(0)
            w, refs_out = refs[len(rows_used)], refs[len(rows_used) + 1 :]
            for n, (name, low) in enumerate(zip(names, starts)):

                @pl.when((step >= low) & (step < low + tiles[name]))
                def _(n=n, name=name):
                    at = 2 * kinds.index(name[0])
                    refs_out[2 * n][...] = mm(refs[at][...], w[...]).astype(bf16)
                    refs_out[2 * n + 1][...] = mm(refs[at + 1][...], w[...]).astype(bf16)

        got = run(
            body,
            (sum(tiles[name] for name in names),),
            [(rows, kept_block(rows.shape)) for rows in rows_used]
            + [(w_out, pl.BlockSpec((w_out.shape[0], unit), lambda i: (0, base + i)))],
            outs,
            marks,
            mib=50,
        )
        for n, name in enumerate(names):
            partial[name] = (got[2 * n], got[2 * n + 1])
        return [got[-2]]

    def begin(name, marks=None):
        kept, out = partial.pop(name)
        if marks:
            out = gated(out, marks)
        flying[name] = swap(out, "tp", stages[name[0]][0])
        values[name] = kept

    def second(names, marks):
        parts = adds([[(values.pop(name), flying.pop(name))] for name in names], marks)
        for name, (out, kept) in zip(names, parts):
            flying[name] = swap(out, "tp", stages[name[0]][1])
            values[name] = kept
        return [parts[0][0]]

    def third(names, marks):
        ((out, kept),) = adds([[(values.pop(name), flying.pop(name)) for name in names]], marks)
        flying[names] = swap(out, "tp", far[0])
        values[names] = kept
        return [out]

    def finish(names, marks):
        kept, got = values.pop(names), flying.pop(names)
        for bit in far[1:]:
            ((out, kept),) = adds([[(kept, got)]], marks)
            got = swap(out, "tp", bit)
        span = slice(spans[names[0]].start, spans[names[-1]].stop)
        wide = block_of(span, 1280)
        low = span.start // wide
        here = pl.BlockSpec((tok_rows, wide), lambda i: (0, low + i))
        part = pl.BlockSpec((tok_rows, wide), lambda i: (0, i))

        def body(kept, got, residual, *refs):
            refs[-2][...] = (residual[...].astype(f32) + (kept[...] + got[...].astype(f32))).astype(bf16)
            refs[-1][...] = jnp.zeros((8, 128), f32)

        before = [(hidden.pop(), ANY)] if hidden else []
        out, mark = run(
            body,
            ((span.stop - span.start) // wide,),
            [(kept, part), (got, part), (residual, here)] + before,
            [(((tok_rows, width), bf16), here), (((8, 128), f32), whole((8, 128)))],
            marks,
            {3: 0} if before else None,
        )
        hidden.append(out)
        return [mark]

    window = onehot[:, :, :tp_count]
    member = jnp.any(window, axis=1).astype(jnp.int32)
    slot_rank = jnp.cumsum(member, axis=0) - member
    slot_ids = jnp.arange(CAP, dtype=jnp.int32)[None, :, None]
    slot_pick = (member.T[:, None, :] == 1) & (slot_rank.T[:, None, :] == slot_ids)
    pick = slot_pick.reshape(first, tok_rows).astype(bf16)

    lanes = 128
    choice_cols = jnp.pad(choices.astype(bf16), ((0, 0), (0, lanes - top)))
    gain = norm_gain[None]

    marks = bulk(("y0",), [])
    begin("y0")
    marks = bulk(("z0",), marks)
    begin("z0")
    marks = bulk(("y1",), marks)
    marks = second(("y0",), marks)
    begin("y1", marks)
    marks = second(("z0",), marks + [pick, choice_cols, gain])
    marks = bulk(("y2",), marks + count_hop())
    marks = second(("y1",), marks)
    marks = third(("y0",), marks)
    marks = third(("z0",), marks)
    begin("y2", marks)
    marks = bulk(("y3",), marks)
    begin("y3")
    marks = third(("y1",), marks)
    marks = finish(("y0",), marks)
    marks = finish(("z0",), marks)
    marks = second(("y2",), marks + count_hop())
    marks = bulk(("y4",), marks)
    begin("y4")
    marks = finish(("y1",), marks)
    marks = third(("y2",), marks)
    router_part = router_payload()
    marks = second(("y3",), marks + [router_part])
    marks = bulk(("y5",), marks)
    begin("y5")
    marks = finish(("y2",), marks)
    marks = third(("y3",), marks)
    marks = second(("y4",), marks)
    marks = finish(("y3",), marks)
    marks = third(("y4",), marks)
    marks = second(("y5",), marks)
    router_all = router_gather(router_part, marks)
    marks = third(("y5",), marks)
    marks = finish(("y4",), marks)
    finish(("y5",), marks)
    (hidden_out,) = hidden

    def norm_body(pick, rows, gain, choice, out):
        stream = mm(pick[...], rows[...])
        scaled = stream * lax.rsqrt(jnp.mean(stream * stream, axis=-1, keepdims=True) + norm_eps)
        out[:, :width] = (scaled * gain[...].astype(f32)).astype(bf16)
        out[:, width:] = mm(pick[...], choice[...]).astype(bf16)

    (normed,) = run(
        norm_body,
        (1,),
        [
            (pick, whole(pick.shape)),
            (hidden_out, whole(hidden_out.shape)),
            (gain, whole((1, width))),
            (choice_cols, whole(choice_cols.shape)),
        ],
        [(((first, width + lanes), bf16), whole((first, width + lanes)))],
        [],
    )
    landed = lax.all_to_all(
        normed.reshape(tp_count, CAP, width + lanes), "tp", split_axis=0, concat_axis=0, tiled=True
    ).reshape(first, width + lanes)
    picked = [landed]
    for bit in ep_bits[::-1]:
        picked = picked + [swap(rows, "ep", bit) for rows in picked]
    rows_all = first * ep_count
    hid = w_gate.shape[2]
    deep = block_of(slice(0, width), 1024)
    last_step = width // deep - 1

    cut = rows_all // 2

    def expert_body(*refs):
        rows, refs = refs[:ep_count], refs[ep_count:]
        gate_a, gate_b, up_a, up_b, down_a, down_b, out, kept, gate_sum, up_sum, active = refs
        step = pl.program_id(0)

        @pl.when(step == 0)
        def _():
            gate_sum[...] = jnp.zeros_like(gate_sum)
            up_sum[...] = jnp.zeros_like(up_sum)

        @pl.when(step <= last_step)
        def _():
            x = jnp.concatenate([r[...] for r in rows], axis=0)
            gate_sum[...] += mm(x[:, : deep // 2], gate_a[0]) + mm(x[:, deep // 2 :], gate_b[0])
            up_sum[...] += mm(x[:, : deep // 2], up_a[0]) + mm(x[:, deep // 2 :], up_b[0])

        @pl.when(step == last_step)
        def _():
            gate = gate_sum[...]
            active[...] = (gate / (1.0 + jnp.exp(-gate)) * up_sum[...]).astype(bf16)

        @pl.when(step > last_step)
        def _():
            x = active[...]
            value = mm(x[:, : hid // 2], down_a[0]) + mm(x[:, hid // 2 :], down_b[0])
            kept[...] = value[:cut]
            out[...] = value[cut:].astype(bf16)

    def early_step(i):
        return jnp.minimum(i, last_step)

    def late_step(i):
        return jnp.maximum(i - last_step - 1, 0)

    deep_rows = pl.BlockSpec((first, deep), lambda i: (0, early_step(i)))
    deep_a = pl.BlockSpec((1, deep // 2, hid), lambda i: (0, 2 * early_step(i), 0))
    deep_b = pl.BlockSpec((1, deep // 2, hid), lambda i: (0, 2 * early_step(i) + 1, 0))
    down_a = pl.BlockSpec((1, hid // 2, deep), lambda i: (0, 0, late_step(i)))
    down_b = pl.BlockSpec((1, hid // 2, deep), lambda i: (0, 1, late_step(i)))
    wide_half = pl.BlockSpec((cut, deep), lambda i: (0, late_step(i)))
    out, kept = run(
        expert_body,
        (2 * (last_step + 1),),
        [(rows, deep_rows) for rows in picked]
        + [(w_gate, deep_a), (w_gate, deep_b), (w_up, deep_a), (w_up, deep_b), (w_down, down_a), (w_down, down_b)],
        [(((cut, width), bf16), wide_half), (((cut, width), f32), wide_half)],
        [],
        scratch=[pltpu.VMEM((rows_all, hid), f32)] * 2 + [pltpu.VMEM((rows_all, hid), bf16)],
        mib=50,
    )
    got = swap(out, "ep", ep_bits[0])

    row_of = jnp.arange(per_part, dtype=jnp.int32)
    column_ids = (jnp.array(rel, jnp.int32) ^ me)[:, None] * per_device + ep_me * per_part + row_of
    column_ids = column_ids.reshape(1, -1)

    def score_body(*refs):
        rows, (table, columns, expert, out) = refs[:ep_count], refs[ep_count:]
        x = jnp.concatenate([r[:, :width] for r in rows], axis=0)
        ids = jnp.concatenate([r[:, width:] for r in rows], axis=0).astype(f32).astype(jnp.int32)
        scores = 1.0 / (1.0 + jnp.exp(-mm_t(x, table[:, :width])))
        here = columns[...]
        chosen = jnp.where(here == expert[...], scores, 0.0)
        total = jnp.zeros_like(scores)
        for k in range(top):
            total += jnp.where(here == ids[:, k : k + 1], scores, 0.0)
        lane = lax.broadcasted_iota(jnp.int32, out.shape, 1)
        chosen = jnp.sum(chosen, axis=-1, keepdims=True)
        total = jnp.sum(total, axis=-1, keepdims=True)
        out[...] = jnp.where(lane == 0, chosen, jnp.where(lane == 1, total, 0.0))

    expert_id = jnp.full((1, 1), me, jnp.int32)
    (parts,) = run(
        score_body,
        (1,),
        [(rows, whole(rows.shape)) for rows in picked]
        + [
            (router_all, whole(router_all.shape)),
            (column_ids, whole(column_ids.shape)),
            (expert_id, whole((1, 1))),
        ],
        [(((rows_all, lanes), f32), whole((rows_all, lanes)))],
        [],
    )
    for bit in ep_bits:
        low = parts.shape[0] // 2
        parts = parts[:low] + swap(parts[low:], "ep", bit)
    for bit in ep_bits[1:]:
        ((out, kept),) = adds([[(kept, got)]], [])
        got = swap(out, "ep", bit)

    def weigh_body(kept, got, part, out):
        value = (kept[...] + got[...].astype(f32)).astype(bf16).astype(f32)
        out[...] = (value * (route_scale * part[:, 0:1] / part[:, 1:2])).astype(bf16)

    (summed,) = run(
        weigh_body,
        (1,),
        [(kept, whole(kept.shape)), (got, whole(kept.shape)), (parts, whole(parts.shape))],
        [((kept.shape, bf16), whole(kept.shape))],
        [],
    )
    returned = lax.all_to_all(
        summed.reshape(tp_count, CAP, width), "tp", split_axis=0, concat_axis=0, tiled=True
    ).reshape(first, width)
    moe_out = mm_rows(pick, returned).astype(bf16)

    digits = router_all[:, width:].reshape(tp_count, per_part * digit_cols)[:, : 2 * routed]
    digits = jnp.sum(digits.astype(jnp.int32), axis=0).reshape(2, routed)
    counts = digits[0] * base_digit + digits[1]
    all_slots = all_rows * ep_count * top
    load = counts.astype(f32) * routed / all_slots
    bias_next = router_bias + bias_rate * jnp.sign(all_slots - counts * routed).astype(f32)
    return (hidden_out, moe_out, load, bias_next)


def solution(mesh):
    placed = (
        P("ep", "tp"),
        P(("ep", "tp"), None),
        P("tp", None),
        P(),
        P(None, "tp"),
        P(),
        P(("ep", "tp"), None),
        P("tp", None, "ep"),
        P("tp", None, "ep"),
        P("tp", "ep", None),
    )
    return jax.shard_map(
        on_device,
        mesh=mesh,
        in_specs=placed,
        out_specs=(P(("ep", "tp"), None), P(("ep", "tp"), None), P(), P()),
        check_vma=False,
    )
```

```python
import jax
import jax.numpy as jnp
from jax import lax
from jax.experimental import pallas as pl
from jax.experimental.pallas import tpu as pltpu
from jax.sharding import PartitionSpec as P

TOP = 8
CAP = 2


norm_eps = 1e-06
route_scale = 2.5
bias_rate = 0.001
f32 = jnp.float32
bf16 = jnp.bfloat16


def swap(value, axis, bit):
    size = lax.axis_size(axis)
    return lax.ppermute(value, axis, [(i, i ^ bit) for i in range(size)])


def bits_of(size):
    return [1 << k for k in range(size.bit_length() - 1)]


def halving_order(stages):
    order = [0]
    for bit in reversed(stages):
        order = order + [j | bit for j in order]
    return order


ANY = pl.BlockSpec(memory_space=pl.ANY)


def run(body, grid, ins, outs, marks, aliases=None, scratch=(), mib=16, moved=1):
    count, skip = len(ins), len(marks)

    def inner(*refs):
        body(*refs[:count], *refs[count + skip :])

    return pl.pallas_call(
        inner,
        grid=grid,
        in_specs=[spec for _, spec in ins] + [ANY] * skip,
        out_specs=[spec for _, spec in outs],
        out_shape=[jax.ShapeDtypeStruct(shape, kind) for (shape, kind), _ in outs],
        input_output_aliases=aliases or {},
        scratch_shapes=list(scratch),
        compiler_params=pltpu.CompilerParams(vmem_limit_bytes=mib * 1024 * 1024),
        cost_estimate=pl.CostEstimate(flops=1, bytes_accessed=moved, transcendentals=0),
    )(*[a for a, _ in ins], *marks)


def whole(shape):
    return pl.BlockSpec(shape, lambda i: (0,) * len(shape))


def kept_block(shape):
    return pl.BlockSpec(shape, lambda i: (0,) * len(shape), pipeline_mode=pl.Buffered(1))


def block_of(span, most):
    size = span.stop - span.start
    best = 128
    for n in range(128, most + 1, 128):
        if size % n == 0 and span.start % n == 0:
            best = n
    return best


def gated(value, marks):
    return run(lambda *refs: None, (1,), [(value, ANY)], [((value.shape, value.dtype), ANY)], marks, {0: 0})[0]


def adds(groups, marks):
    rows = groups[0][0][0].shape[0]
    cut = rows // 2
    plain = all(len(group) == 1 for group in groups)
    sizes = {kept.shape[1] for group in groups for kept, _ in group}
    wide = block_of(slice(0, min(sizes)), 640) if plain and len(sizes) == 1 and cut >= 128 else None
    ins, outs = [], []
    for group in groups:
        cols = sum(kept.shape[1] for kept, _ in group)
        for pair in group:
            for value in pair:
                ins.append((value, pl.BlockSpec((rows, wide), lambda i: (0, i)) if wide else whole(value.shape)))
        for kind in (bf16, f32):
            spec = pl.BlockSpec((cut, wide), lambda i: (0, i)) if wide else whole((cut, cols))
            outs.append((((cut, cols), kind), spec))
    counts = [len(group) for group in groups]

    def body(*refs):
        place, out_place = 0, 2 * sum(counts)
        for count in counts:
            out, rest = refs[out_place], refs[out_place + 1]
            low = 0
            for _ in range(count):
                kept, got = refs[place], refs[place + 1]
                size = kept.shape[1]
                out[:, low : low + size] = (kept[cut:].astype(f32) + got[cut:].astype(f32)).astype(bf16)
                rest[:, low : low + size] = kept[:cut].astype(f32) + got[:cut].astype(f32)
                low += size
                place += 2
            out_place += 2

    got = run(body, (min(sizes) // wide if wide else 1,), ins, outs, marks)
    return [(got[2 * n], got[2 * n + 1]) for n in range(len(groups))]


def mm(a, b):
    return jnp.dot(a, b, preferred_element_type=f32)


def mm_t(a, b):
    return lax.dot_general(a, b, (((1,), (1,)), ((), ())), preferred_element_type=f32)


def mm_rows(a, b):
    return lax.dot_general(a, b, (((0,), (0,)), ((), ())), preferred_element_type=f32)


def on_device(
    attn_out, residual, w_out, norm_gain, router, router_bias, choices, w_gate, w_up, w_down
):
    tp_count = lax.axis_size("tp")
    ep_count = lax.axis_size("ep")
    tok_rows = residual.shape[0]
    width = residual.shape[1]
    routed = router_bias.shape[0]
    top = choices.shape[1]
    all_rows = tp_count * tok_rows
    first = CAP * tp_count
    me = lax.axis_index("tp")
    ep_me = lax.axis_index("ep")
    tp_bits, ep_bits = bits_of(tp_count), bits_of(ep_count)
    y_first = list(tp_bits)
    z_first = [tp_bits[1], tp_bits[0]] + tp_bits[2:]
    far = tp_bits[2:]
    stages = {"y": y_first, "z": z_first}
    order = {"y": halving_order(y_first), "z": halving_order(z_first)}
    half = all_rows // 2
    flying, values, hidden = {}, {}, []

    onehot = choices[:, :, None] == jnp.arange(routed, dtype=jnp.int32)
    counts = jnp.sum(onehot.astype(jnp.int32), axis=(0, 1))
    count_hops = list(ep_bits)
    rel = [0]
    for bit in tp_bits[::-1]:
        rel = rel + [j | bit for j in rel]
    per_device = routed // tp_count
    per_part = per_device // ep_count
    digit_cols = -(-2 * routed // (per_part * 128)) * 128
    base_digit = 64

    def count_hop():
        nonlocal counts
        counts = counts + swap(counts, "ep", count_hops.pop(0))
        return [counts]

    def router_payload():
        part = lax.dynamic_slice_in_dim(router.T, ep_me * per_part, per_part, axis=0)
        digits = jnp.concatenate([counts // base_digit, counts % base_digit]).astype(bf16)
        digits = jnp.pad(digits, (0, per_part * digit_cols - 2 * routed)).reshape(per_part, digit_cols)
        return jnp.concatenate([part, digits], axis=1)

    def router_gather(part, marks):
        part = gated(part, marks)
        for bit in tp_bits[::-1]:
            part = jnp.concatenate([part, swap(part, "tp", bit)], axis=0)
        return part

    blocks = [
        lax.dynamic_slice_in_dim(attn_out, (me ^ j) * tok_rows, tok_rows, axis=0)
        for j in range(tp_count)
    ]
    halves = {
        kind: [
            jnp.concatenate([blocks[j] for j in order[kind][part]], axis=0)
            for part in (slice(0, tp_count // 2), slice(tp_count // 2, tp_count))
        ]
        for kind in ("y", "z")
    }
    tiles = {"y0": 2, "z0": 4, "y1": 4, "y2": 6, "y3": 5, "y4": 4, "y5": 3}
    unit = width // sum(tiles.values())
    spans, lo = {}, 0
    for name, count in tiles.items():
        spans[name] = slice(lo, lo + count * unit)
        lo += count * unit
    partial = {}

    def bulk(names, marks):
        base = spans[names[0]].start // unit
        starts = [spans[name].start // unit - base for name in names]
        outs = []
        for name, low in zip(names, starts):
            top_block = tiles[name] - 1
            spec = pl.BlockSpec(
                (half, unit), lambda i, low=low, top_block=top_block: (0, jnp.clip(i - low, 0, top_block))
            )
            outs += [(((half, tiles[name] * unit), bf16), spec)] * 2

        kinds = sorted({name[0] for name in names})
        rows_used = [rows for kind in kinds for rows in halves[kind]]

        def body(*refs):
            step = pl.program_id(0)
            w, refs_out = refs[len(rows_used)], refs[len(rows_used) + 1 :]
            for n, (name, low) in enumerate(zip(names, starts)):

                @pl.when((step >= low) & (step < low + tiles[name]))
                def _(n=n, name=name):
                    at = 2 * kinds.index(name[0])
                    refs_out[2 * n][...] = mm(refs[at][...], w[...]).astype(bf16)
                    refs_out[2 * n + 1][...] = mm(refs[at + 1][...], w[...]).astype(bf16)

        got = run(
            body,
            (sum(tiles[name] for name in names),),
            [(rows, kept_block(rows.shape)) for rows in rows_used]
            + [(w_out, pl.BlockSpec((w_out.shape[0], unit), lambda i: (0, base + i)))],
            outs,
            marks,
            mib=50,
        )
        for n, name in enumerate(names):
            partial[name] = (got[2 * n], got[2 * n + 1])
        return [got[-2]]

    def begin(name, marks=None):
        kept, out = partial.pop(name)
        if marks:
            out = gated(out, marks)
        flying[name] = swap(out, "tp", stages[name[0]][0])
        values[name] = kept

    def second(names, marks):
        parts = adds([[(values.pop(name), flying.pop(name))] for name in names], marks)
        for name, (out, kept) in zip(names, parts):
            flying[name] = swap(out, "tp", stages[name[0]][1])
            values[name] = kept
        return [parts[0][0]]

    def third(names, marks):
        ((out, kept),) = adds([[(values.pop(name), flying.pop(name)) for name in names]], marks)
        flying[names] = swap(out, "tp", far[0])
        values[names] = kept
        return [out]

    def finish(names, marks):
        kept, got = values.pop(names), flying.pop(names)
        for bit in far[1:]:
            ((out, kept),) = adds([[(kept, got)]], marks)
            got = swap(out, "tp", bit)
        span = slice(spans[names[0]].start, spans[names[-1]].stop)
        wide = block_of(span, 1280)
        low = span.start // wide
        here = pl.BlockSpec((tok_rows, wide), lambda i: (0, low + i))
        part = pl.BlockSpec((tok_rows, wide), lambda i: (0, i))

        def body(kept, got, residual, *refs):
            refs[-2][...] = (residual[...].astype(f32) + (kept[...] + got[...].astype(f32))).astype(bf16)
            refs[-1][...] = jnp.zeros((8, 128), f32)

        before = [(hidden.pop(), ANY)] if hidden else []
        out, mark = run(
            body,
            ((span.stop - span.start) // wide,),
            [(kept, part), (got, part), (residual, here)] + before,
            [(((tok_rows, width), bf16), here), (((8, 128), f32), whole((8, 128)))],
            marks,
            {3: 0} if before else None,
        )
        hidden.append(out)
        return [mark]

    window = onehot[:, :, :tp_count]
    member = jnp.any(window, axis=1).astype(jnp.int32)
    slot_rank = jnp.cumsum(member, axis=0) - member
    slot_ids = jnp.arange(CAP, dtype=jnp.int32)[None, :, None]
    slot_pick = (member.T[:, None, :] == 1) & (slot_rank.T[:, None, :] == slot_ids)
    pick = slot_pick.reshape(first, tok_rows).astype(bf16)

    lanes = 128
    choice_cols = jnp.pad(choices.astype(bf16), ((0, 0), (0, lanes - top)))
    gain = norm_gain[None]

    marks = bulk(("y0",), [])
    begin("y0")
    marks = bulk(("z0",), marks)
    begin("z0")
    marks = bulk(("y1",), marks)
    marks = second(("y0",), marks)
    begin("y1", marks)
    marks = second(("z0",), marks + [pick, choice_cols, gain])
    marks = bulk(("y2",), marks + count_hop())
    marks = second(("y1",), marks)
    marks = third(("y0",), marks)
    marks = third(("z0",), marks)
    begin("y2", marks)
    marks = bulk(("y3",), marks)
    begin("y3")
    marks = third(("y1",), marks)
    marks = finish(("y0",), marks)
    marks = finish(("z0",), marks)
    marks = second(("y2",), marks + count_hop())
    marks = bulk(("y4",), marks)
    begin("y4")
    marks = finish(("y1",), marks)
    marks = third(("y2",), marks)
    router_part = router_payload()
    marks = second(("y3",), marks + [router_part])
    marks = bulk(("y5",), marks)
    begin("y5")
    marks = finish(("y2",), marks)
    marks = third(("y3",), marks)
    marks = second(("y4",), marks)
    marks = third(("y4",), marks)
    marks = finish(("y3",), marks)
    marks = second(("y5",), marks)
    marks = third(("y5",), marks)
    router_all = router_gather(router_part, marks)
    marks = finish(("y4",), marks)
    finish(("y5",), marks)
    (hidden_out,) = hidden

    def norm_body(pick, rows, gain, choice, out):
        stream = mm(pick[...], rows[...])
        scaled = stream * lax.rsqrt(jnp.mean(stream * stream, axis=-1, keepdims=True) + norm_eps)
        out[:, :width] = (scaled * gain[...].astype(f32)).astype(bf16)
        out[:, width:] = mm(pick[...], choice[...]).astype(bf16)

    (normed,) = run(
        norm_body,
        (1,),
        [
            (pick, whole(pick.shape)),
            (hidden_out, whole(hidden_out.shape)),
            (gain, whole((1, width))),
            (choice_cols, whole(choice_cols.shape)),
        ],
        [(((first, width + lanes), bf16), whole((first, width + lanes)))],
        [],
    )
    landed = lax.all_to_all(
        normed.reshape(tp_count, CAP, width + lanes), "tp", split_axis=0, concat_axis=0, tiled=True
    ).reshape(first, width + lanes)
    picked = [landed]
    for bit in ep_bits[::-1]:
        picked = picked + [swap(rows, "ep", bit) for rows in picked]
    rows_all = first * ep_count
    hid = w_gate.shape[2]
    deep = block_of(slice(0, width), 1024)
    last_step = width // deep - 1

    cut = rows_all // 2

    def expert_body(*refs):
        rows, refs = refs[:ep_count], refs[ep_count:]
        gate_a, gate_b, up_a, up_b, down_a, down_b, out, kept, gate_sum, up_sum, active = refs
        step = pl.program_id(0)

        @pl.when(step == 0)
        def _():
            gate_sum[...] = jnp.zeros_like(gate_sum)
            up_sum[...] = jnp.zeros_like(up_sum)

        @pl.when(step <= last_step)
        def _():
            x = jnp.concatenate([r[...] for r in rows], axis=0)
            gate_sum[...] += mm(x[:, : deep // 2], gate_a[0]) + mm(x[:, deep // 2 :], gate_b[0])
            up_sum[...] += mm(x[:, : deep // 2], up_a[0]) + mm(x[:, deep // 2 :], up_b[0])

        @pl.when(step == last_step)
        def _():
            gate = gate_sum[...]
            active[...] = (gate / (1.0 + jnp.exp(-gate)) * up_sum[...]).astype(bf16)

        @pl.when(step > last_step)
        def _():
            x = active[...]
            value = mm(x[:, : hid // 2], down_a[0]) + mm(x[:, hid // 2 :], down_b[0])
            kept[...] = value[:cut]
            out[...] = value[cut:].astype(bf16)

    def early_step(i):
        return jnp.minimum(i, last_step)

    def late_step(i):
        return jnp.maximum(i - last_step - 1, 0)

    deep_rows = pl.BlockSpec((first, deep), lambda i: (0, early_step(i)))
    deep_a = pl.BlockSpec((1, deep // 2, hid), lambda i: (0, 2 * early_step(i), 0))
    deep_b = pl.BlockSpec((1, deep // 2, hid), lambda i: (0, 2 * early_step(i) + 1, 0))
    down_a = pl.BlockSpec((1, hid // 2, deep), lambda i: (0, 0, late_step(i)))
    down_b = pl.BlockSpec((1, hid // 2, deep), lambda i: (0, 1, late_step(i)))
    wide_half = pl.BlockSpec((cut, deep), lambda i: (0, late_step(i)))
    out, kept = run(
        expert_body,
        (2 * (last_step + 1),),
        [(rows, deep_rows) for rows in picked]
        + [(w_gate, deep_a), (w_gate, deep_b), (w_up, deep_a), (w_up, deep_b), (w_down, down_a), (w_down, down_b)],
        [(((cut, width), bf16), wide_half), (((cut, width), f32), wide_half)],
        [],
        scratch=[pltpu.VMEM((rows_all, hid), f32)] * 2 + [pltpu.VMEM((rows_all, hid), bf16)],
        mib=50,
    )
    got = swap(out, "ep", ep_bits[0])

    row_of = jnp.arange(per_part, dtype=jnp.int32)
    column_ids = (jnp.array(rel, jnp.int32) ^ me)[:, None] * per_device + ep_me * per_part + row_of
    column_ids = column_ids.reshape(1, -1)

    def score_body(*refs):
        rows, (table, columns, expert, out) = refs[:ep_count], refs[ep_count:]
        x = jnp.concatenate([r[:, :width] for r in rows], axis=0)
        ids = jnp.concatenate([r[:, width:] for r in rows], axis=0).astype(f32).astype(jnp.int32)
        scores = 1.0 / (1.0 + jnp.exp(-mm_t(x, table[:, :width])))
        here = columns[...]
        chosen = jnp.where(here == expert[...], scores, 0.0)
        total = jnp.zeros_like(scores)
        for k in range(top):
            total += jnp.where(here == ids[:, k : k + 1], scores, 0.0)
        lane = lax.broadcasted_iota(jnp.int32, out.shape, 1)
        chosen = jnp.sum(chosen, axis=-1, keepdims=True)
        total = jnp.sum(total, axis=-1, keepdims=True)
        out[...] = jnp.where(lane == 0, chosen, jnp.where(lane == 1, total, 0.0))

    expert_id = jnp.full((1, 1), me, jnp.int32)
    (parts,) = run(
        score_body,
        (1,),
        [(rows, whole(rows.shape)) for rows in picked]
        + [
            (router_all, whole(router_all.shape)),
            (column_ids, whole(column_ids.shape)),
            (expert_id, whole((1, 1))),
        ],
        [(((rows_all, lanes), f32), whole((rows_all, lanes)))],
        [],
    )
    for bit in ep_bits:
        low = parts.shape[0] // 2
        parts = parts[:low] + swap(parts[low:], "ep", bit)
    for bit in ep_bits[1:]:
        ((out, kept),) = adds([[(kept, got)]], [])
        got = swap(out, "ep", bit)

    def weigh_body(kept, got, part, out):
        value = (kept[...] + got[...].astype(f32)).astype(bf16).astype(f32)
        out[...] = (value * (route_scale * part[:, 0:1] / part[:, 1:2])).astype(bf16)

    (summed,) = run(
        weigh_body,
        (1,),
        [(kept, whole(kept.shape)), (got, whole(kept.shape)), (parts, whole(parts.shape))],
        [((kept.shape, bf16), whole(kept.shape))],
        [],
    )
    returned = lax.all_to_all(
        summed.reshape(tp_count, CAP, width), "tp", split_axis=0, concat_axis=0, tiled=True
    ).reshape(first, width)
    moe_out = mm_rows(pick, returned).astype(bf16)

    digits = router_all[:, width:].reshape(tp_count, per_part * digit_cols)[:, : 2 * routed]
    digits = jnp.sum(digits.astype(jnp.int32), axis=0).reshape(2, routed)
    counts = digits[0] * base_digit + digits[1]
    all_slots = all_rows * ep_count * top
    load = counts.astype(f32) * routed / all_slots
    bias_next = router_bias + bias_rate * jnp.sign(all_slots - counts * routed).astype(f32)
    return (hidden_out, moe_out, load, bias_next)


def solution(mesh):
    placed = (
        P("ep", "tp"),
        P(("ep", "tp"), None),
        P("tp", None),
        P(),
        P(None, "tp"),
        P(),
        P(("ep", "tp"), None),
        P("tp", None, "ep"),
        P("tp", None, "ep"),
        P("tp", "ep", None),
    )
    return jax.shard_map(
        on_device,
        mesh=mesh,
        in_specs=placed,
        out_specs=(P(("ep", "tp"), None), P(("ep", "tp"), None), P(), P()),
        check_vma=False,
    )
```

```python
import jax
import jax.numpy as jnp
from jax import lax
from jax.experimental import pallas as pl
from jax.experimental.pallas import tpu as pltpu
from jax.sharding import PartitionSpec as P

TOP = 8
CAP = 2


norm_eps = 1e-06
route_scale = 2.5
bias_rate = 0.001
f32 = jnp.float32
bf16 = jnp.bfloat16


def swap(value, axis, bit):
    size = lax.axis_size(axis)
    return lax.ppermute(value, axis, [(i, i ^ bit) for i in range(size)])


def bits_of(size):
    return [1 << k for k in range(size.bit_length() - 1)]


def halving_order(stages):
    order = [0]
    for bit in reversed(stages):
        order = order + [j | bit for j in order]
    return order


ANY = pl.BlockSpec(memory_space=pl.ANY)


def run(body, grid, ins, outs, marks, aliases=None, scratch=(), mib=16, moved=1):
    count, skip = len(ins), len(marks)

    def inner(*refs):
        body(*refs[:count], *refs[count + skip :])

    return pl.pallas_call(
        inner,
        grid=grid,
        in_specs=[spec for _, spec in ins] + [ANY] * skip,
        out_specs=[spec for _, spec in outs],
        out_shape=[jax.ShapeDtypeStruct(shape, kind) for (shape, kind), _ in outs],
        input_output_aliases=aliases or {},
        scratch_shapes=list(scratch),
        compiler_params=pltpu.CompilerParams(vmem_limit_bytes=mib * 1024 * 1024),
        cost_estimate=pl.CostEstimate(flops=1, bytes_accessed=moved, transcendentals=0),
    )(*[a for a, _ in ins], *marks)


def whole(shape):
    return pl.BlockSpec(shape, lambda i: (0,) * len(shape))


def kept_block(shape):
    return pl.BlockSpec(shape, lambda i: (0,) * len(shape), pipeline_mode=pl.Buffered(1))


def block_of(span, most):
    size = span.stop - span.start
    best = 128
    for n in range(128, most + 1, 128):
        if size % n == 0 and span.start % n == 0:
            best = n
    return best


def gated(value, marks):
    return run(lambda *refs: None, (1,), [(value, ANY)], [((value.shape, value.dtype), ANY)], marks, {0: 0})[0]


def adds(groups, marks):
    rows = groups[0][0][0].shape[0]
    cut = rows // 2
    plain = all(len(group) == 1 for group in groups)
    sizes = {kept.shape[1] for group in groups for kept, _ in group}
    wide = block_of(slice(0, min(sizes)), 640) if plain and len(sizes) == 1 and cut >= 128 else None
    ins, outs = [], []
    for group in groups:
        cols = sum(kept.shape[1] for kept, _ in group)
        for pair in group:
            for value in pair:
                ins.append((value, pl.BlockSpec((rows, wide), lambda i: (0, i)) if wide else whole(value.shape)))
        for kind in (bf16, f32):
            spec = pl.BlockSpec((cut, wide), lambda i: (0, i)) if wide else whole((cut, cols))
            outs.append((((cut, cols), kind), spec))
    counts = [len(group) for group in groups]

    def body(*refs):
        place, out_place = 0, 2 * sum(counts)
        for count in counts:
            out, rest = refs[out_place], refs[out_place + 1]
            low = 0
            for _ in range(count):
                kept, got = refs[place], refs[place + 1]
                size = kept.shape[1]
                out[:, low : low + size] = (kept[cut:].astype(f32) + got[cut:].astype(f32)).astype(bf16)
                rest[:, low : low + size] = kept[:cut].astype(f32) + got[:cut].astype(f32)
                low += size
                place += 2
            out_place += 2

    got = run(body, (min(sizes) // wide if wide else 1,), ins, outs, marks)
    return [(got[2 * n], got[2 * n + 1]) for n in range(len(groups))]


def mm(a, b):
    return jnp.dot(a, b, preferred_element_type=f32)


def mm_t(a, b):
    return lax.dot_general(a, b, (((1,), (1,)), ((), ())), preferred_element_type=f32)


def mm_rows(a, b):
    return lax.dot_general(a, b, (((0,), (0,)), ((), ())), preferred_element_type=f32)


def on_device(
    attn_out, residual, w_out, norm_gain, router, router_bias, choices, w_gate, w_up, w_down
):
    tp_count = lax.axis_size("tp")
    ep_count = lax.axis_size("ep")
    tok_rows = residual.shape[0]
    width = residual.shape[1]
    routed = router_bias.shape[0]
    top = choices.shape[1]
    all_rows = tp_count * tok_rows
    first = CAP * tp_count
    me = lax.axis_index("tp")
    ep_me = lax.axis_index("ep")
    tp_bits, ep_bits = bits_of(tp_count), bits_of(ep_count)
    y_first = list(tp_bits)
    z_first = [tp_bits[1], tp_bits[0]] + tp_bits[2:]
    far = tp_bits[2:]
    stages = {"y": y_first, "z": z_first}
    order = {"y": halving_order(y_first), "z": halving_order(z_first)}
    half = all_rows // 2
    flying, values, hidden = {}, {}, []

    onehot = choices[:, :, None] == jnp.arange(routed, dtype=jnp.int32)
    counts = jnp.sum(onehot.astype(jnp.int32), axis=(0, 1))
    count_hops = list(ep_bits)
    rel = [0]
    for bit in tp_bits[::-1]:
        rel = rel + [j | bit for j in rel]
    per_device = routed // tp_count
    per_part = per_device // ep_count
    digit_cols = -(-2 * routed // (per_part * 128)) * 128
    base_digit = 64

    def count_hop():
        nonlocal counts
        counts = counts + swap(counts, "ep", count_hops.pop(0))
        return [counts]

    def router_payload():
        part = lax.dynamic_slice_in_dim(router.T, ep_me * per_part, per_part, axis=0)
        digits = jnp.concatenate([counts // base_digit, counts % base_digit]).astype(bf16)
        digits = jnp.pad(digits, (0, per_part * digit_cols - 2 * routed)).reshape(per_part, digit_cols)
        return jnp.concatenate([part, digits], axis=1)

    def router_gather(part, marks):
        part = gated(part, marks)
        for bit in tp_bits[::-1]:
            part = jnp.concatenate([part, swap(part, "tp", bit)], axis=0)
        return part

    blocks = [
        lax.dynamic_slice_in_dim(attn_out, (me ^ j) * tok_rows, tok_rows, axis=0)
        for j in range(tp_count)
    ]
    halves = {
        kind: [
            jnp.concatenate([blocks[j] for j in order[kind][part]], axis=0)
            for part in (slice(0, tp_count // 2), slice(tp_count // 2, tp_count))
        ]
        for kind in ("y", "z")
    }
    tiles = {"y0": 3, "z0": 4, "y1": 4, "y2": 6, "y3": 5, "y4": 4, "y5": 2}
    unit = width // sum(tiles.values())
    spans, lo = {}, 0
    for name, count in tiles.items():
        spans[name] = slice(lo, lo + count * unit)
        lo += count * unit
    partial = {}

    def bulk(names, marks):
        base = spans[names[0]].start // unit
        starts = [spans[name].start // unit - base for name in names]
        outs = []
        for name, low in zip(names, starts):
            top_block = tiles[name] - 1
            spec = pl.BlockSpec(
                (half, unit), lambda i, low=low, top_block=top_block: (0, jnp.clip(i - low, 0, top_block))
            )
            outs += [(((half, tiles[name] * unit), bf16), spec)] * 2

        kinds = sorted({name[0] for name in names})
        rows_used = [rows for kind in kinds for rows in halves[kind]]

        def body(*refs):
            step = pl.program_id(0)
            w, refs_out = refs[len(rows_used)], refs[len(rows_used) + 1 :]
            for n, (name, low) in enumerate(zip(names, starts)):

                @pl.when((step >= low) & (step < low + tiles[name]))
                def _(n=n, name=name):
                    at = 2 * kinds.index(name[0])
                    refs_out[2 * n][...] = mm(refs[at][...], w[...]).astype(bf16)
                    refs_out[2 * n + 1][...] = mm(refs[at + 1][...], w[...]).astype(bf16)

        got = run(
            body,
            (sum(tiles[name] for name in names),),
            [(rows, kept_block(rows.shape)) for rows in rows_used]
            + [(w_out, pl.BlockSpec((w_out.shape[0], unit), lambda i: (0, base + i)))],
            outs,
            marks,
            mib=50,
        )
        for n, name in enumerate(names):
            partial[name] = (got[2 * n], got[2 * n + 1])
        return [got[-2]]

    def begin(name, marks=None):
        kept, out = partial.pop(name)
        if marks:
            out = gated(out, marks)
        flying[name] = swap(out, "tp", stages[name[0]][0])
        values[name] = kept

    def second(names, marks):
        parts = adds([[(values.pop(name), flying.pop(name))] for name in names], marks)
        for name, (out, kept) in zip(names, parts):
            flying[name] = swap(out, "tp", stages[name[0]][1])
            values[name] = kept
        return [parts[0][0]]

    def third(names, marks):
        ((out, kept),) = adds([[(values.pop(name), flying.pop(name)) for name in names]], marks)
        flying[names] = swap(out, "tp", far[0])
        values[names] = kept
        return [out]

    def finish(names, marks):
        kept, got = values.pop(names), flying.pop(names)
        for bit in far[1:]:
            ((out, kept),) = adds([[(kept, got)]], marks)
            got = swap(out, "tp", bit)
        span = slice(spans[names[0]].start, spans[names[-1]].stop)
        wide = block_of(span, 1280)
        low = span.start // wide
        here = pl.BlockSpec((tok_rows, wide), lambda i: (0, low + i))
        part = pl.BlockSpec((tok_rows, wide), lambda i: (0, i))

        def body(kept, got, residual, *refs):
            refs[-2][...] = (residual[...].astype(f32) + (kept[...] + got[...].astype(f32))).astype(bf16)
            refs[-1][...] = jnp.zeros((8, 128), f32)

        before = [(hidden.pop(), ANY)] if hidden else []
        out, mark = run(
            body,
            ((span.stop - span.start) // wide,),
            [(kept, part), (got, part), (residual, here)] + before,
            [(((tok_rows, width), bf16), here), (((8, 128), f32), whole((8, 128)))],
            marks,
            {3: 0} if before else None,
        )
        hidden.append(out)
        return [mark]

    window = onehot[:, :, :tp_count]
    member = jnp.any(window, axis=1).astype(jnp.int32)
    slot_rank = jnp.cumsum(member, axis=0) - member
    slot_ids = jnp.arange(CAP, dtype=jnp.int32)[None, :, None]
    slot_pick = (member.T[:, None, :] == 1) & (slot_rank.T[:, None, :] == slot_ids)
    pick = slot_pick.reshape(first, tok_rows).astype(bf16)

    lanes = 128
    choice_cols = jnp.pad(choices.astype(bf16), ((0, 0), (0, lanes - top)))
    gain = norm_gain[None]

    marks = bulk(("y0",), [])
    begin("y0")
    marks = bulk(("z0",), marks)
    begin("z0")
    marks = bulk(("y1",), marks)
    marks = second(("y0",), marks)
    begin("y1", marks)
    marks = second(("z0",), marks + [pick, choice_cols, gain])
    marks = bulk(("y2",), marks + count_hop())
    marks = second(("y1",), marks)
    marks = third(("y0",), marks)
    marks = third(("z0",), marks)
    begin("y2", marks)
    marks = bulk(("y3",), marks)
    begin("y3")
    marks = third(("y1",), marks)
    marks = finish(("y0",), marks)
    marks = finish(("z0",), marks)
    marks = second(("y2",), marks + count_hop())
    marks = bulk(("y4",), marks)
    begin("y4")
    marks = finish(("y1",), marks)
    marks = third(("y2",), marks)
    router_part = router_payload()
    marks = second(("y3",), marks + [router_part])
    marks = bulk(("y5",), marks)
    begin("y5")
    marks = finish(("y2",), marks)
    marks = third(("y3",), marks)
    marks = second(("y4",), marks)
    marks = finish(("y3",), marks)
    marks = third(("y4",), marks)
    marks = second(("y5",), marks)
    router_all = router_gather(router_part, marks)
    marks = third(("y5",), marks)
    marks = finish(("y4",), marks)
    finish(("y5",), marks)
    (hidden_out,) = hidden

    def norm_body(pick, rows, gain, choice, out):
        stream = mm(pick[...], rows[...])
        scaled = stream * lax.rsqrt(jnp.mean(stream * stream, axis=-1, keepdims=True) + norm_eps)
        out[:, :width] = (scaled * gain[...].astype(f32)).astype(bf16)
        out[:, width:] = mm(pick[...], choice[...]).astype(bf16)

    (normed,) = run(
        norm_body,
        (1,),
        [
            (pick, whole(pick.shape)),
            (hidden_out, whole(hidden_out.shape)),
            (gain, whole((1, width))),
            (choice_cols, whole(choice_cols.shape)),
        ],
        [(((first, width + lanes), bf16), whole((first, width + lanes)))],
        [],
    )
    landed = lax.all_to_all(
        normed.reshape(tp_count, CAP, width + lanes), "tp", split_axis=0, concat_axis=0, tiled=True
    ).reshape(first, width + lanes)
    picked = [landed]
    for bit in ep_bits[::-1]:
        picked = picked + [swap(rows, "ep", bit) for rows in picked]
    rows_all = first * ep_count
    hid = w_gate.shape[2]
    deep = block_of(slice(0, width), 1024)
    last_step = width // deep - 1

    cut = rows_all // 2

    def expert_body(*refs):
        rows, refs = refs[:ep_count], refs[ep_count:]
        gate_a, gate_b, up_a, up_b, down_a, down_b, out, kept, gate_sum, up_sum, active = refs
        step = pl.program_id(0)

        @pl.when(step == 0)
        def _():
            gate_sum[...] = jnp.zeros_like(gate_sum)
            up_sum[...] = jnp.zeros_like(up_sum)

        @pl.when(step <= last_step)
        def _():
            x = jnp.concatenate([r[...] for r in rows], axis=0)
            gate_sum[...] += mm(x[:, : deep // 2], gate_a[0]) + mm(x[:, deep // 2 :], gate_b[0])
            up_sum[...] += mm(x[:, : deep // 2], up_a[0]) + mm(x[:, deep // 2 :], up_b[0])

        @pl.when(step == last_step)
        def _():
            gate = gate_sum[...]
            active[...] = (gate / (1.0 + jnp.exp(-gate)) * up_sum[...]).astype(bf16)

        @pl.when(step > last_step)
        def _():
            x = active[...]
            value = mm(x[:, : hid // 2], down_a[0]) + mm(x[:, hid // 2 :], down_b[0])
            kept[...] = value[:cut]
            out[...] = value[cut:].astype(bf16)

    def early_step(i):
        return jnp.minimum(i, last_step)

    def late_step(i):
        return jnp.maximum(i - last_step - 1, 0)

    deep_rows = pl.BlockSpec((first, deep), lambda i: (0, early_step(i)))
    deep_a = pl.BlockSpec((1, deep // 2, hid), lambda i: (0, 2 * early_step(i), 0))
    deep_b = pl.BlockSpec((1, deep // 2, hid), lambda i: (0, 2 * early_step(i) + 1, 0))
    down_a = pl.BlockSpec((1, hid // 2, deep), lambda i: (0, 0, late_step(i)))
    down_b = pl.BlockSpec((1, hid // 2, deep), lambda i: (0, 1, late_step(i)))
    wide_half = pl.BlockSpec((cut, deep), lambda i: (0, late_step(i)))
    out, kept = run(
        expert_body,
        (2 * (last_step + 1),),
        [(rows, deep_rows) for rows in picked]
        + [(w_gate, deep_a), (w_gate, deep_b), (w_up, deep_a), (w_up, deep_b), (w_down, down_a), (w_down, down_b)],
        [(((cut, width), bf16), wide_half), (((cut, width), f32), wide_half)],
        [],
        scratch=[pltpu.VMEM((rows_all, hid), f32)] * 2 + [pltpu.VMEM((rows_all, hid), bf16)],
        mib=50,
    )
    got = swap(out, "ep", ep_bits[0])

    row_of = jnp.arange(per_part, dtype=jnp.int32)
    column_ids = (jnp.array(rel, jnp.int32) ^ me)[:, None] * per_device + ep_me * per_part + row_of
    column_ids = column_ids.reshape(1, -1)

    def score_body(*refs):
        rows, (table, columns, expert, out) = refs[:ep_count], refs[ep_count:]
        x = jnp.concatenate([r[:, :width] for r in rows], axis=0)
        ids = jnp.concatenate([r[:, width:] for r in rows], axis=0).astype(f32).astype(jnp.int32)
        scores = 1.0 / (1.0 + jnp.exp(-mm_t(x, table[:, :width])))
        here = columns[...]
        chosen = jnp.where(here == expert[...], scores, 0.0)
        total = jnp.zeros_like(scores)
        for k in range(top):
            total += jnp.where(here == ids[:, k : k + 1], scores, 0.0)
        lane = lax.broadcasted_iota(jnp.int32, out.shape, 1)
        chosen = jnp.sum(chosen, axis=-1, keepdims=True)
        total = jnp.sum(total, axis=-1, keepdims=True)
        out[...] = jnp.where(lane == 0, chosen, jnp.where(lane == 1, total, 0.0))

    expert_id = jnp.full((1, 1), me, jnp.int32)
    (parts,) = run(
        score_body,
        (1,),
        [(rows, whole(rows.shape)) for rows in picked]
        + [
            (router_all, whole(router_all.shape)),
            (column_ids, whole(column_ids.shape)),
            (expert_id, whole((1, 1))),
        ],
        [(((rows_all, lanes), f32), whole((rows_all, lanes)))],
        [],
    )
    for bit in ep_bits:
        low = parts.shape[0] // 2
        parts = parts[:low] + swap(parts[low:], "ep", bit)
    for bit in ep_bits[1:]:
        ((out, kept),) = adds([[(kept, got)]], [])
        got = swap(out, "ep", bit)

    def weigh_body(kept, got, part, out):
        value = (kept[...] + got[...].astype(f32)).astype(bf16).astype(f32)
        out[...] = (value * (route_scale * part[:, 0:1] / part[:, 1:2])).astype(bf16)

    (summed,) = run(
        weigh_body,
        (1,),
        [(kept, whole(kept.shape)), (got, whole(kept.shape)), (parts, whole(parts.shape))],
        [((kept.shape, bf16), whole(kept.shape))],
        [],
    )
    returned = lax.all_to_all(
        summed.reshape(tp_count, CAP, width), "tp", split_axis=0, concat_axis=0, tiled=True
    ).reshape(first, width)
    moe_out = mm_rows(pick, returned).astype(bf16)

    digits = router_all[:, width:].reshape(tp_count, per_part * digit_cols)[:, : 2 * routed]
    digits = jnp.sum(digits.astype(jnp.int32), axis=0).reshape(2, routed)
    counts = digits[0] * base_digit + digits[1]
    all_slots = all_rows * ep_count * top
    load = counts.astype(f32) * routed / all_slots
    bias_next = router_bias + bias_rate * jnp.sign(all_slots - counts * routed).astype(f32)
    return (hidden_out, moe_out, load, bias_next)


def solution(mesh):
    placed = (
        P("ep", "tp"),
        P(("ep", "tp"), None),
        P("tp", None),
        P(),
        P(None, "tp"),
        P(),
        P(("ep", "tp"), None),
        P("tp", None, "ep"),
        P("tp", None, "ep"),
        P("tp", "ep", None),
    )
    return jax.shard_map(
        on_device,
        mesh=mesh,
        in_specs=placed,
        out_specs=(P(("ep", "tp"), None), P(("ep", "tp"), None), P(), P()),
        check_vma=False,
    )
```
